512 devices in a mesh: seq: 16 (over z), exp: 32 (over y, x, core).
Axes of the slice: x: 4, y: 4, z: 16, core: 2. Of those that a mesh axis runs over, the one named last changes fastest.
Arguments:
- adjoint: bfloat16 [2048, 2880], P('seq'), may hold values from -6 to 6
- seed_grad: float32 [2048, 2880], P('seq', 'exp'), may hold values from -3 to 3
- layer_input: bfloat16 [2048, 2880], P('seq'), may hold values from -6 to 6
- norm_gain: float32 [2880], replicated, may hold values from 0.5 to 1.5
- router_weight: bfloat16 [2880, 32], replicated, may hold values from -0.109375 to 0.109375
- routes: int32 [2048, 4], P('seq'), may hold values from 0 to 31, all different within a row; in each aligned block of 128 rows (0 to 127, 128 to 255, ...) at most 32 rows name the same one
- expert_out: bfloat16 [2048, 4, 2880], P('seq', None, 'exp'), may hold values from -6 to 6
- stored_query: bfloat16 [2048, 2048], P('seq', 'exp'), may hold values from -3 to 3
- stored_key: bfloat16 [2048, 256], P('seq'), may hold values from -3 to 3
- stored_value: bfloat16 [2048, 256], P('seq'), may hold values from -6 to 6
- query_weight: bfloat16 [2880, 2048], P(None, 'exp'), may hold values from -0.109375 to 0.109375
- key_weight: bfloat16 [2880, 256], P('exp'), may hold values from -0.109375 to 0.109375
- value_weight: bfloat16 [2880, 256], P('exp'), may hold values from -0.109375 to 0.109375
- output_weight: bfloat16 [2048, 2880], P('exp'), may hold values from -0.125 to 0.125
- gate_weight: bfloat16 [32, 2880, 1536], P('exp', None, 'seq'), may hold values from -0.109375 to 0.109375
- up_weight: bfloat16 [32, 2880, 1536], P('exp', None, 'seq'), may hold values from -0.109375 to 0.109375
- down_weight: bfloat16 [32, 1536, 2880], P('exp', 'seq'), may hold values from -0.15625 to 0.15625
- stored_gate: bfloat16 [32, 512, 1536], P('exp', None, 'seq'), may hold values from -8 to 8
- stored_up: bfloat16 [32, 512, 1536], P('exp', None, 'seq'), may hold values from -6 to 6
Outputs:
- new_adjoint: float32 [2048, 2880], P('seq', 'exp')
The draws below stay inside these ranges and needn't reach their ends.
Inputs may be any that keep to these rules, and one draw needn't show every extreme that they name: `routes`: in each block of 128 consecutive tokens every expert is named by at most 32 tokens, and some block names some expert 32 times.
All inputs are finite; a program needn't handle non-finite values.
Results may differ from the reference program's by a relative error of at most 0.019.
Values may be sent and summed in bfloat16 or wider, within the bound.
No kernel may reach another device: no remote copies, remote signals or barrier semaphores. Data moves between devices by JAX's collectives and lax.ppermute only.
A program may use at most 64 MiB of HBM per device.

```python
import math
import jax
import jax.numpy as jnp
import numpy as np
from jax import lax

D = 2880
HEAD_DIM = 64
TOPK = 4
WINDOW = 128
QH = 32
KVH = 4
FF = 1536
TOK_DEV = 128
EXPERTS = 32
CAP = 32
TOKENS = 2048
SLOTS = 512
N_SEQ = 16


def steps_of(stream_key, extent, cuts, low, largest):
    gain = 1.0
    for position, blocks in cuts:
        steps = jax.random.uniform(jax.random.fold_in(jax.random.fold_in(stream_key, 6), position), (blocks,), jnp.float32, low / len(cuts), largest / len(cuts))
        gain = gain * jnp.repeat(jnp.exp(steps), extent[position] // blocks).reshape((-1,) + (1,) * (len(extent) - 1 - position))
    return gain


def routed_block(key, own, number, rows, number_of, top, reach, skew):
    sequence = jax.random.permutation(key, number_of)
    packed, common = load_shares(number_of, rows * top, reach, skew, True), load_shares(number_of, rows * top, reach, skew, False)
    places = jnp.arange(number_of)

    def named(lengths, rotation):
        used = int((lengths > 0).sum())
        fixed = max(1, used // 4)
        moved = fixed + (places - fixed + rotation * (used - fixed)) % max(1, number_of - fixed)
        return jnp.zeros((number_of,), jnp.int32).at[sequence[jnp.where(places < fixed, places, moved)]].set(jnp.asarray(lengths, jnp.int32))

    lengths = jnp.where(number % 4 == 0, named(packed, number // 4), named(common, number - number // 4 - 1))
    mixed = jax.random.permutation(jax.random.fold_in(own, 3), number_of)
    source_of, sink = mixed[0:number_of // 2 * 2:2], mixed[1:number_of // 2 * 2:2]
    room = jnp.minimum(lengths[source_of] - 1, reach - lengths[sink]) // 2
    room = jnp.where((source_of == sequence[0]) | (sink == sequence[0]) | (lengths[sink] == 0), 0, jnp.maximum(room, 0))
    moved = jax.random.randint(jax.random.fold_in(own, 4), (number_of // 2,), 0, 1 << 20) % (room + 1)
    lengths = lengths.at[source_of].add(-moved).at[sink].add(moved)
    members = jnp.searchsorted(jnp.cumsum(lengths), jnp.arange(rows * top), side="right").astype(jnp.int32)
    table = members.reshape(top, rows).T
    table = table[jax.random.permutation(jax.random.fold_in(own, 1), rows)]
    rotation = jax.random.randint(jax.random.fold_in(own, 2), (rows, 1), 0, top)
    return jnp.take_along_axis(table, (jnp.arange(top)[None, :] + rotation) % top, axis=1)


def load_shares(number_of, total, limit, lean, full):
    portions = [(1 << 20) // math.isqrt(rank ** lean) + 1 for rank in range(1, number_of + 1)]
    largest = limit if full else min(limit, max(-(-total // number_of), total * portions[0] // sum(portions)))
    least = 1 if total - largest >= number_of - 1 else 0
    given, spare = [largest] + [least] * (number_of - 1), total - largest - least * (number_of - 1)
    while spare > 0:
        movable = [i for i in range(1, number_of) if given[i] < largest] or [i for i in range(1, number_of) if given[i] < limit]
        pool, budget = sum([portions[i] for i in movable]), spare
        for i in movable:
            addition = min(limit - given[i], max(1, budget * portions[i] // pool), spare)
            given[i] = given[i] + addition
            spare = spare - addition
    return np.array(given)


def scatter_about(key, extent, deviation, reach, split=(), kind=jnp.bfloat16):
    drawn = deviation * jax.random.normal(key, extent, jnp.float32)
    if split:
        drawn = drawn * steps_of(key, extent, split, -0.22, 0.18)
    return jnp.clip(drawn, -reach, reach).astype(kind)


def setup_inputs(seed: int = 0) -> dict:
    key_of = jax.random.split(jax.random.key(seed), 20)
    adjoint = scatter_about(key_of[0], (TOKENS, D), 1.0, 6.0, ((0, 16),))
    seed_grad = scatter_about(key_of[1], (TOKENS, D), 0.5, 3.0, ((0, 16), (1, 32)), jnp.float32)
    layer_input = scatter_about(key_of[2], (TOKENS, D), 1.0, 6.0, ((0, 16),))
    norm_gain = jnp.clip(1.0 + 0.1 * jax.random.normal(key_of[3], (D,), jnp.float32), 0.5, 1.5)
    router_weight = scatter_about(key_of[4], (D, EXPERTS), D ** -0.5, 0.109375)
    routes_keys = jax.random.split(jax.random.fold_in(key_of[5], 1), TOKENS // TOK_DEV)
    routes_turns = jax.random.permutation(jax.random.fold_in(key_of[5], 3), TOKENS // TOK_DEV)
    routes = jax.vmap(lambda own, number: routed_block(jax.random.fold_in(key_of[5], 2), own, number, TOK_DEV, EXPERTS, TOPK, CAP, 2))(routes_keys, routes_turns).reshape((TOKENS, TOPK))
    expert_out = scatter_about(key_of[6], (TOKENS, TOPK, D), 1.0, 6.0, ((0, 16), (2, 32)))
    stored_query = scatter_about(key_of[7], (TOKENS, QH * HEAD_DIM), 1.0, 3.0, ((0, 16), (1, 32)))
    stored_key = scatter_about(key_of[8], (TOKENS, KVH * HEAD_DIM), 1.0, 3.0, ((0, 16),))
    stored_value = scatter_about(key_of[9], (TOKENS, KVH * HEAD_DIM), 1.0, 6.0, ((0, 16),))
    query_weight = scatter_about(key_of[10], (D, QH * HEAD_DIM), D ** -0.5, 0.109375, ((1, 32),))
    key_weight = scatter_about(key_of[11], (D, KVH * HEAD_DIM), D ** -0.5, 0.109375, ((0, 32),))
    value_weight = scatter_about(key_of[12], (D, KVH * HEAD_DIM), D ** -0.5, 0.109375, ((0, 32),))
    output_weight = scatter_about(key_of[13], (QH * HEAD_DIM, D), (QH * HEAD_DIM) ** -0.5, 0.125, ((0, 32),))
    gate_weight = scatter_about(key_of[14], (EXPERTS, D, FF), D ** -0.5, 0.109375, ((0, 32), (2, 16)))
    up_weight = scatter_about(key_of[15], (EXPERTS, D, FF), D ** -0.5, 0.109375, ((0, 32), (2, 16)))
    down_weight = scatter_about(key_of[16], (EXPERTS, FF, D), FF ** -0.5, 0.15625, ((0, 32), (1, 16)))
    stored_gate = scatter_about(key_of[17], (EXPERTS, SLOTS, FF), 1.5, 8.0, ((0, 32), (2, 16)))
    stored_up = scatter_about(key_of[18], (EXPERTS, SLOTS, FF), 1.0, 6.0, ((0, 32), (2, 16)))
    return dict(adjoint=adjoint, seed_grad=seed_grad, layer_input=layer_input, norm_gain=norm_gain, router_weight=router_weight, routes=routes, expert_out=expert_out, stored_query=stored_query, stored_key=stored_key, stored_value=stored_value, query_weight=query_weight, key_weight=key_weight, value_weight=value_weight, output_weight=output_weight, gate_weight=gate_weight, up_weight=up_weight, down_weight=down_weight, stored_gate=stored_gate, stored_up=stored_up)


EPSILON = 1e-05
PRECISE = lax.Precision.HIGHEST

def norm_parts(layer_input, norm_gain):
    values = layer_input.astype(jnp.float32)
    inverse = lax.rsqrt(lax.optimization_barrier(jnp.mean(values * values, axis=-1, keepdims=True)) + EPSILON)
    return (values, inverse, values * inverse * norm_gain)

def float_dot(left, right):
    return jnp.dot(left.astype(jnp.float32), right.astype(jnp.float32), precision=PRECISE)

def held_round(array):
    return lax.optimization_barrier(array.astype(jnp.bfloat16)).astype(jnp.float32)

def reference(adjoint, seed_grad, layer_input, norm_gain, router_weight, routes, expert_out, stored_query, stored_key, stored_value, query_weight, key_weight, value_weight, output_weight, gate_weight, up_weight, down_weight, stored_gate, stored_up):
    tokens_all = adjoint.shape[0]
    blocks = tokens_all // TOK_DEV
    adjoint_float = adjoint.astype(jnp.float32)
    values, inverse, normed = norm_parts(layer_input, norm_gain)
    logits = jnp.dot(normed.astype(jnp.bfloat16), router_weight, preferred_element_type=jnp.float32)
    chosen = jnp.take_along_axis(logits, routes, axis=1)
    raised = jnp.exp(chosen)
    shares = raised / lax.optimization_barrier(jnp.sum(raised, axis=1, keepdims=True))
    aligned = lax.optimization_barrier(jnp.sum(adjoint_float[:, None, :] * expert_out.astype(jnp.float32), axis=2))
    logit_back = shares * (aligned - lax.optimization_barrier(jnp.sum(shares * aligned, axis=1, keepdims=True)))
    picked = jax.nn.one_hot(routes, EXPERTS, dtype=jnp.float32)
    coef_rows = lax.optimization_barrier(jnp.sum(logit_back[:, :, None] * picked, axis=1))
    router_back = jnp.dot(coef_rows, router_weight.astype(jnp.float32).T, precision=PRECISE)
    route_gate = shares.astype(jnp.bfloat16)
    scaled = (route_gate.astype(jnp.float32)[:, :, None] * adjoint_float[:, None, :]).astype(jnp.bfloat16)
    counts = lax.optimization_barrier(jnp.sum(jax.nn.one_hot(routes, EXPERTS, dtype=jnp.int32), axis=1))
    counts = counts.reshape(blocks, TOK_DEV, EXPERTS)
    earlier = (jnp.cumsum(counts, axis=1) - counts).reshape(tokens_all, EXPERTS)
    slot_rank = jnp.take_along_axis(earlier, routes, axis=1)
    block_index = (jnp.arange(tokens_all, dtype=jnp.int32) // TOK_DEV)[:, None]
    slot_index = (routes * SLOTS + block_index * CAP + slot_rank).astype(jnp.int32)
    expert_rows = jnp.zeros((EXPERTS * SLOTS, D), jnp.bfloat16)
    expert_rows = expert_rows.at[slot_index.reshape(-1)].set(scaled.reshape(-1, D))
    expert_rows = expert_rows.reshape(EXPERTS, SLOTS, D)
    band = FF // N_SEQ

    def expert_back(operands):
        rows, gate_w, up_w, down_w, gate_store, up_store = operands
        hidden_back = float_dot(rows, down_w.T)
        gate_vals = gate_store.astype(jnp.float32)
        sigma = jax.nn.sigmoid(gate_vals)
        gate_back = (hidden_back * up_store.astype(jnp.float32) * (sigma * (1.0 + gate_vals * (1.0 - sigma)))).astype(jnp.bfloat16)
        up_back = (hidden_back * (gate_vals * sigma)).astype(jnp.bfloat16)
        summed = jnp.zeros((rows.shape[0], D), jnp.float32)
        for part_index in range(N_SEQ):
            lower = part_index * band
            upper = lower + band
            band_sum = float_dot(gate_back[:, lower:upper], gate_w[:, lower:upper].T)
            band_sum = band_sum + float_dot(up_back[:, lower:upper], up_w[:, lower:upper].T)
            summed = summed + held_round(band_sum)
        return summed
    expert_sums = lax.map(expert_back, (expert_rows, gate_weight, up_weight, down_weight, stored_gate, stored_up))
    moe_back = lax.optimization_barrier(jnp.sum(expert_sums.reshape(EXPERTS * SLOTS, D)[slot_index], axis=1))
    group_size = QH // KVH
    score_scale = HEAD_DIM ** (-0.5)
    positions = jnp.arange(tokens_all, dtype=jnp.int32)
    visible = (positions[:, None] >= positions[None, :]) & (positions[:, None] - positions[None, :] < WINDOW)

    def head_step(total, head):
        kv_start = head // group_size * HEAD_DIM
        query_head = lax.dynamic_slice_in_dim(stored_query, head * HEAD_DIM, HEAD_DIM, 1).astype(jnp.float32)
        key_head = lax.dynamic_slice_in_dim(stored_key, kv_start, HEAD_DIM, 1).astype(jnp.float32)
        value_head = lax.dynamic_slice_in_dim(stored_value, kv_start, HEAD_DIM, 1).astype(jnp.float32)
        out_rows = lax.dynamic_slice_in_dim(output_weight, head * HEAD_DIM, HEAD_DIM, 0).astype(jnp.float32)
        query_proj = lax.dynamic_slice_in_dim(query_weight, head * HEAD_DIM, HEAD_DIM, 1).astype(jnp.float32)
        key_proj = lax.dynamic_slice_in_dim(key_weight, kv_start, HEAD_DIM, 1).astype(jnp.float32)
        value_proj = lax.dynamic_slice_in_dim(value_weight, kv_start, HEAD_DIM, 1).astype(jnp.float32)
        out_back = held_round(jnp.dot(adjoint_float, out_rows.T, precision=PRECISE))
        scores = jnp.dot(query_head, key_head.T, precision=PRECISE) * score_scale
        raised_scores = jnp.where(visible, jnp.exp(scores), 0.0)
        soft_rows = raised_scores / lax.optimization_barrier(jnp.sum(raised_scores, axis=1, keepdims=True))
        value_grad = held_round(jnp.dot(held_round(soft_rows).T, out_back, precision=PRECISE))
        attn_back = jnp.dot(out_back, value_head.T, precision=PRECISE)
        score_back = held_round(soft_rows * (attn_back - lax.optimization_barrier(jnp.sum(soft_rows * attn_back, axis=1, keepdims=True))))
        query_grad = held_round(jnp.dot(score_back, key_head, precision=PRECISE) * score_scale)
        key_grad = held_round(jnp.dot(score_back.T, query_head, precision=PRECISE) * score_scale)
        total = total + jnp.dot(query_grad, query_proj.T, precision=PRECISE)
        total = total + jnp.dot(key_grad, key_proj.T, precision=PRECISE)
        total = total + jnp.dot(value_grad, value_proj.T, precision=PRECISE)
        return (total, None)
    attention_back, _ = lax.scan(head_step, jnp.zeros((tokens_all, D), jnp.float32), jnp.arange(QH, dtype=jnp.int32))
    lifted = norm_gain * (router_back + moe_back + attention_back)
    mean_term = lax.optimization_barrier(jnp.mean(values * lifted, axis=-1, keepdims=True))
    return seed_grad + adjoint_float + inverse * lifted - values * inverse ** 3 * mean_term
```

```python
import jax
import jax.numpy as jnp
from jax import lax
from jax.experimental import pallas as pl
from jax.experimental.pallas import tpu as pltpu
from jax.sharding import Mesh
from jax.sharding import PartitionSpec as P

D = 2880
HEAD_DIM = 64
WINDOW = 128
QH = 32
KVH = 4
TOPK = 4
EXPERTS = 32
CAP = 32
TOK = 128
BAND = 96
HALF = BAND // 2
COLS = D // 32
PART = 96
SENDERS = D // PART
BLOCKS = 8
MINE = BLOCKS * CAP
EPSILON = 1e-05
SCALE = HEAD_DIM ** (-0.5)

BF = jnp.bfloat16
F32 = jnp.float32
SEQ = ("zh", "zl")


def dot(left, right, contract=((1,), (0,))):
    return lax.dot_general(left, right, (contract, ((), ())), preferred_element_type=F32)


def rows_of(shape):
    return lax.broadcasted_iota(jnp.int32, shape, 0)


def lanes_of(shape):
    return lax.broadcasted_iota(jnp.int32, shape, 1)


def split(value):
    high = value.astype(BF)
    return high, (value - high.astype(F32)).astype(BF)


def whole(shape_dtypes, flops=0, moved=0):
    return dict(
        out_shape=[jax.ShapeDtypeStruct(s, d) for s, d in shape_dtypes],
        compiler_params=pltpu.CompilerParams(vmem_limit_bytes=40 * 1024 * 1024),
        cost_estimate=pl.CostEstimate(flops=flops, bytes_accessed=moved, transcendentals=0),
    )


SMEM = pl.BlockSpec(memory_space=pltpu.SMEM)
VMEM = pl.BlockSpec(memory_space=pltpu.VMEM)


def route_kernel(where, layer, gain, router, routes, adjoint, out_w, pay, inverse, shares, out_back):
    values = layer[...].astype(F32)
    inv = lax.rsqrt(jnp.sum(values * values, axis=0, keepdims=True) / D + EPSILON)
    inverse[...] = inv
    high, low = split(router[...].astype(F32) * gain[...])
    logits = (dot(high, layer[...]) + dot(low, layer[...])) * inv
    names = rows_of((EXPERTS, TOK))
    picked = [names == routes[k : k + 1, :] for k in range(TOPK)]
    raised = [
        jnp.exp(jnp.sum(jnp.where(p, logits, 0.0), axis=0, keepdims=True)) for p in picked
    ]
    total = raised[0] + raised[1] + raised[2] + raised[3]
    taken = sum(p.astype(F32) for p in picked)
    earlier = (rows_of((TOK, TOK)) < lanes_of((TOK, TOK))).astype(BF)
    ranks = dot(taken.astype(BF), earlier)
    line = rows_of((16, TOK))
    meta = jnp.zeros((16, TOK), F32)
    for k in range(TOPK):
        share = raised[k] / total
        shares[k : k + 1, :] = share
        rank = jnp.sum(jnp.where(picked[k], ranks, 0.0), axis=0, keepdims=True)
        meta = jnp.where(line == k, routes[k : k + 1, :].astype(F32), meta)
        meta = jnp.where(line == TOPK + k, rank, meta)
        meta = jnp.where(line == 2 * TOPK + k, share, meta)
    start = pl.multiple_of(jnp.minimum(where[0], SENDERS - 1) * PART, PART)
    pay[0:PART, :] = adjoint[pl.ds(start, PART), :]
    pay[PART:, :] = meta.astype(BF)
    out_back[...] = dot(out_w[...], adjoint[...]).astype(BF)


def pack_kernel(where, down, gate, up, store_g, store_u, query_w, to_next, to_prev, own_g, own_u, query_parts):
    def chosen(parity):
        i, j = rows_of((16 * CAP, MINE)), lanes_of((16 * CAP, MINE))
        return (i == (2 * (j // CAP) + parity) * CAP + j % CAP).astype(BF)

    parity = where[1]
    here, there = chosen(parity), chosen(1 - parity)
    own_g[...] = dot(store_g[...], here).astype(BF)
    own_u[...] = dot(store_u[...], here).astype(BF)
    sent_g = dot(store_g[...], there).astype(BF)
    sent_u = dot(store_u[...], there).astype(BF)
    for first, ref in ((HALF, to_next), (0, to_prev)):
        for n, weight in enumerate((down, gate, up)):
            ref[n * HALF : (n + 1) * HALF, :] = weight[first : first + HALF, :]
        ref[3 * HALF :, :] = jnp.zeros((16, D), BF)
        for n, sent in enumerate((sent_g, sent_u)):
            for m in range(3):
                lane = (3 * n + m) * MINE
                ref[3 * HALF :, lane : lane + MINE] = sent[first + 16 * m : first + 16 * m + 16, :]
    for c in range(32):
        piece = query_w[:, c * COLS : (c + 1) * COLS]
        query_parts[c, :, :] = jnp.zeros((32, 256), BF)
        query_parts[c, :, 0:COLS] = piece[0:32]
        query_parts[c, :, 128 : 128 + COLS] = piece[32:64]


def attend_kernel(where, query, out_back, kv, kv_prev, next_q, aligned, grads):
    block = where[2]
    key_at, query_at = rows_of((TOK, TOK)), lanes_of((TOK, TOK))
    same = key_at <= query_at
    before = key_at > query_at

    def rows(q, out, before_kv, same_kv, before_mask):
        def half(kv_rows, mask):
            scores = dot(kv_rows[:, :HEAD_DIM], q) * SCALE
            return jnp.where(mask, jnp.exp(scores), 0.0), dot(kv_rows[:, HEAD_DIM:], out)

        p_before, a_before = half(before_kv, before_mask)
        p_same, a_same = half(same_kv, same)
        total = jnp.sum(p_before, axis=0, keepdims=True) + jnp.sum(p_same, axis=0, keepdims=True)
        p_before, p_same = p_before / total, p_same / total
        mean = jnp.sum(p_before * a_before, axis=0, keepdims=True) + jnp.sum(
            p_same * a_same, axis=0, keepdims=True
        )
        return (
            p_before.astype(BF),
            (p_before * (a_before - mean)).astype(BF),
            p_same.astype(BF),
            (p_same * (a_same - mean)).astype(BF),
        )

    q, out = query[...], out_back[...]
    own, prev, following = kv[...], kv_prev[...], next_q[TOK:, :]
    q_next, out_next = next_q[0:HEAD_DIM, :], next_q[HEAD_DIM : 2 * HEAD_DIM, :]
    _, sb_prev, p_own, sb_own = rows(q, out, prev, own, before & (block > 0))
    p_next, sb_next, _, _ = rows(q_next, out_next, own, following, before)
    live = jnp.where(block < 15, 1.0, 0.0)
    over = ((0,), (0,))
    across = ((1,), (1,))
    grads[0:64, :] = (
        (dot(prev[:, :HEAD_DIM], sb_prev, over) + dot(own[:, :HEAD_DIM], sb_own, over)) * SCALE
    ).astype(BF)
    grads[64:128, :] = (
        (dot(q, sb_own, across) + live * dot(q_next, sb_next, across)) * SCALE
    ).astype(BF)
    grads[128:192, :] = (dot(out, p_own, across) + live * dot(out_next, p_next, across)).astype(BF)
    line = rows_of((16, TOK))
    tail = jnp.zeros((16, TOK), F32)
    for k in range(TOPK):
        high = aligned[k : k + 1, :].astype(BF).astype(F32)
        tail = jnp.where(line == k, high, tail)
        tail = jnp.where(line == TOPK + k, aligned[k : k + 1, :] - high, tail)
    grads[192:208, :] = tail.astype(BF)


def dispatch_kernel(gathered, query_parts, sent, places, gates):
    names = rows_of((EXPERTS, TOK)).astype(F32)
    for b in range(BLOCKS):
        meta = gathered[b, PART:, :].astype(F32)
        place = jnp.full((EXPERTS, TOK), -1.0, F32)
        gate = jnp.zeros((EXPERTS, TOK), F32)
        for k in range(TOPK):
            match = names == meta[k : k + 1, :]
            place = jnp.where(match, meta[TOPK + k : TOPK + k + 1, :] + CAP * (b % 4), place)
            gate = jnp.where(match, meta[2 * TOPK + k : 2 * TOPK + k + 1, :], gate)
        places[:, b * TOK : (b + 1) * TOK] = place
        gates[:, b * TOK : (b + 1) * TOK] = gate
    features = [
        jnp.concatenate([gathered[b, 0:PART, :] for b in range(4 * h, 4 * h + 4)], axis=1)
        for h in range(2)
    ]
    slot = rows_of((TOK, 4 * TOK)).astype(F32)

    def step(e, carry):
        for h in range(2):
            lanes = slice(h * 4 * TOK, (h + 1) * 4 * TOK)
            placing = jnp.where(
                slot == places[pl.ds(e, 1), lanes], gates[pl.ds(e, 1), lanes], 0.0
            ).astype(BF)
            sent[e, 0:PART, h * TOK : (h + 1) * TOK] = dot(
                features[h], placing, ((1,), (1,))
            ).astype(BF)
        return carry

    lax.fori_loop(0, EXPERTS, step, 0)
    sent[:, PART:, :] = query_parts[...]


def expert_kernel(rows, down, gate, up, own_g, own_u, from_prev, from_next, sent, total):
    features = rows[0:SENDERS, 0:PART, :].reshape(D, MINE)

    def act(hidden, g, u):
        g, u = g.astype(F32), u.astype(F32)
        sigma = jax.nn.sigmoid(g)
        return (
            (hidden * u * (sigma * (1.0 + g * (1.0 - sigma)))).astype(BF),
            (hidden * (g * sigma)).astype(BF),
        )

    def stored(ref, n):
        return jnp.concatenate(
            [ref[3 * HALF :, (3 * n + m) * MINE : (3 * n + m + 1) * MINE] for m in range(3)], axis=0
        )

    backs = list(act(dot(down[...], features), own_g[...], own_u[...]))
    for ref in (from_prev, from_next):
        backs += list(act(dot(ref[0:HALF, :], features), stored(ref, 0), stored(ref, 1)))
    weights = [gate[...], up[...]]
    for ref in (from_prev, from_next):
        weights += [ref[HALF : 2 * HALF, :], ref[2 * HALF : 3 * HALF, :]]
    total[0:D, :] = dot(
        jnp.concatenate(weights, axis=0), jnp.concatenate(backs, axis=0), ((0,), (0,))
    )
    total[D:, :] = jnp.zeros((8, MINE), F32)
    for c in range(32):
        sent[c, :, :] = total[c * COLS : c * COLS + PART, :].astype(BF)


def combine_kernel(returned, places, sent):
    slot = rows_of((TOK, 4 * TOK)).astype(F32)

    for h in range(2):
        lanes = slice(h * 4 * TOK, (h + 1) * 4 * TOK)

        def step(i, total):
            picks, terms = [], []
            for n in range(2):
                e = 2 * i + n
                picks.append((slot == places[pl.ds(e, 1), lanes]).astype(BF))
                terms.append(returned[e, :, h * TOK : (h + 1) * TOK])
            return total + dot(jnp.concatenate(terms, axis=1), jnp.concatenate(picks, axis=0))

        total = lax.fori_loop(0, EXPERTS // 2, step, jnp.zeros((PART, 4 * TOK), F32))
        for b in range(4):
            sent[4 * h + b, :, :] = total[:, b * TOK : (b + 1) * TOK].astype(BF)


def project_kernel(grads, rows, key_w, value_w, router, shares, routes, attended):
    total = jnp.zeros((PART, TOK), F32)
    for h in range(QH):
        for n in range(2):
            weight = rows[h, PART:, n * 128 : n * 128 + PART]
            total = total + dot(weight, grads[h, 32 * n : 32 * n + 32, :], ((0,), (0,)))
    group = QH // KVH
    for first, weight in ((64, key_w), (128, value_w)):
        sums = []
        for g in range(KVH):
            some = grads[g * group, first : first + 64, :].astype(F32)
            for h in range(g * group + 1, (g + 1) * group):
                some = some + grads[h, first : first + 64, :].astype(F32)
            sums.append(some)
        high, low = split(jnp.concatenate(sums, axis=0))
        total = total + dot(weight[...], high) + dot(weight[...], low)
    tail = grads[0, 192:208, :].astype(F32)
    for h in range(1, QH):
        tail = tail + grads[h, 192:208, :].astype(F32)
    aligned = [tail[k : k + 1, :] + tail[TOPK + k : TOPK + k + 1, :] for k in range(TOPK)]
    mean = sum(shares[k : k + 1, :] * aligned[k] for k in range(TOPK))
    names = rows_of((EXPERTS, TOK))
    coef = jnp.zeros((EXPERTS, TOK), F32)
    for k in range(TOPK):
        back = shares[k : k + 1, :] * (aligned[k] - mean)
        coef = jnp.where(names == routes[k : k + 1, :], back, coef)
    high, low = split(coef)
    attended[...] = total + dot(router[...], high) + dot(router[...], low)


def lift_kernel(bands, attended, gain, values, lifted, stat):
    total = attended[...]
    for b in range(BLOCKS):
        total = total + bands[b, :, :].astype(F32)
    total = jnp.where(rows_of((PART, TOK)) < COLS, total, 0.0) * gain[...]
    lifted[...] = total
    stat[...] = jnp.broadcast_to(
        jnp.sum(values[...] * total, axis=0, keepdims=True), (32, TOK)
    )


def finish_kernel(stats, lifted, values, inverse, base, result):
    mean = jnp.sum(stats[...], axis=0, keepdims=True) / D
    inv = inverse[...]
    result[...] = base[...] + (
        inv * lifted[0:COLS, :] - values[0:COLS, :] * (inv * inv * inv * mean)
    )


def on_device(
    adjoint,
    seed_grad,
    layer_input,
    norm_gain,
    router_weight,
    routes,
    expert_out,
    stored_query,
    stored_key,
    stored_value,
    query_weight,
    key_weight,
    value_weight,
    output_weight,
    gate_weight,
    up_weight,
    down_weight,
    stored_gate,
    stored_up,
):
    col = lax.axis_index("exp")
    block = lax.axis_index(SEQ)
    parity = lax.axis_index("zl")
    where = jnp.stack([col, parity, block]).astype(jnp.int32)
    first = col * COLS
    adjoint_t, layer_t, routes_t = adjoint.T, layer_input.T, routes.T
    to_next = [(i, (i + 1) % 16) for i in range(16)]
    to_prev = [(j, i) for i, j in to_next]

    pay, inverse, shares, out_back = pl.pallas_call(
        route_kernel,
        in_specs=[SMEM] + [VMEM] * 6,
        out_specs=[VMEM] * 4,
        **whole([((PART + 16, TOK), BF), ((1, TOK), F32), ((TOPK, TOK), F32), ((HEAD_DIM, TOK), BF)]),
        name="route",
    )(where, layer_t, norm_gain[None, :], router_weight.T, routes_t, adjoint_t, output_weight)
    gathered = lax.all_to_all(
        jnp.broadcast_to(pay[None], (BLOCKS, PART + 16, TOK)), "zh", 0, 0, tiled=True
    )

    kv_start = col // (QH // KVH) * HEAD_DIM
    kv = jnp.concatenate(
        [lax.dynamic_slice_in_dim(a, kv_start, HEAD_DIM, 1) for a in (stored_key, stored_value)], axis=1
    )
    query_t = stored_query.T
    kv_prev = lax.ppermute(kv, SEQ, to_next)
    from_next_q = lax.ppermute(jnp.concatenate([query_t, out_back, kv], axis=0), SEQ, to_prev)

    down, gate, up = down_weight[0], gate_weight[0].T, up_weight[0].T
    wide, narrow = ((3 * HALF + 16, D), BF), ((BAND, MINE), BF)
    w_next, w_prev, own_g, own_u, query_parts = pl.pallas_call(
        pack_kernel,
        in_specs=[SMEM] + [VMEM] * 6,
        out_specs=[VMEM] * 5,
        **whole([wide, wide, narrow, narrow, ((32, 32, 256), BF)]),
        name="pack",
    )(where, down, gate, up, stored_gate[0].T, stored_up[0].T, query_weight.T)
    w_from_prev = lax.ppermute(w_next, SEQ, to_next)
    w_from_next = lax.ppermute(w_prev, SEQ, to_prev)

    adjoint_cols = lax.dynamic_slice_in_dim(adjoint_t, first, COLS, 0).astype(F32)
    values = lax.dynamic_slice_in_dim(layer_t, first, COLS, 0).astype(F32)
    aligned = jnp.sum(adjoint_cols[:, None, :] * expert_out.transpose(2, 1, 0).astype(F32), axis=0)
    (grads,) = pl.pallas_call(
        attend_kernel,
        in_specs=[SMEM] + [VMEM] * 6,
        out_specs=[VMEM],
        **whole([((208, TOK), BF)]),
        name="attend",
    )(where, query_t, out_back, kv, kv_prev, from_next_q, aligned)
    all_grads = lax.all_gather(grads, "exp", axis=0)

    sent, places, _ = pl.pallas_call(
        dispatch_kernel,
        in_specs=[VMEM] * 2,
        out_specs=[VMEM] * 3,
        **whole([((32, PART + 32, MINE), BF), ((EXPERTS, BLOCKS * TOK), F32), ((EXPERTS, BLOCKS * TOK), F32)]),
        name="dispatch",
    )(gathered, query_parts)
    rows = lax.all_to_all(sent, "exp", 0, 0, tiled=True)
    (terms,) = pl.pallas_call(
        expert_kernel,
        in_specs=[VMEM] * 8,
        out_specs=[VMEM],
        scratch_shapes=[pltpu.VMEM((D + 8, MINE), F32)],
        **whole([((32, PART, MINE), BF)]),
        name="expert",
    )(rows, down, gate, up, own_g, own_u, w_from_prev, w_from_next)
    returned = lax.all_to_all(terms, "exp", 0, 0, tiled=True)
    (sums,) = pl.pallas_call(
        combine_kernel,
        in_specs=[VMEM] * 2,
        out_specs=[VMEM],
        **whole([((BLOCKS, PART, TOK), BF)]),
        name="combine",
    )(returned, places)
    bands = lax.all_to_all(sums, "zh", 0, 0, tiled=True)

    pad = ((0, PART - COLS), (0, 0))
    router_cols = jnp.pad(lax.dynamic_slice_in_dim(router_weight, first, COLS, 0), pad)
    gain = jnp.pad(lax.dynamic_slice_in_dim(norm_gain, first, COLS, 0)[:, None], pad)
    values = jnp.pad(values, pad)
    (attended,) = pl.pallas_call(
        project_kernel,
        in_specs=[VMEM] * 7,
        out_specs=[VMEM],
        **whole([((PART, TOK), F32)]),
        name="project",
    )(all_grads, rows, jnp.pad(key_weight, pad), jnp.pad(value_weight, pad), router_cols, shares, routes_t)
    lifted, stat = pl.pallas_call(
        lift_kernel,
        in_specs=[VMEM] * 4,
        out_specs=[VMEM] * 2,
        **whole([((PART, TOK), F32), ((32, TOK), F32)]),
        name="lift",
    )(bands, attended, gain, values)
    stats = lax.all_to_all(stat, "exp", 0, 0, tiled=True)
    (result,) = pl.pallas_call(
        finish_kernel,
        in_specs=[VMEM] * 5,
        out_specs=[VMEM],
        **whole([((COLS, TOK), F32)]),
        name="finish",
    )(stats, lifted, values, inverse, seed_grad.T + adjoint_cols)
    return result.T


def solution(mesh):
    finer = Mesh(mesh.devices.reshape(8, 2, 32), ("zh", "zl", "exp"))
    placed = (
        P(SEQ, None),
        P(SEQ, "exp"),
        P(SEQ, None),
        P(),
        P(),
        P(SEQ, None),
        P(SEQ, None, "exp"),
        P(SEQ, "exp"),
        P(SEQ, None),
        P(SEQ, None),
        P(None, "exp"),
        P("exp", None),
        P("exp", None),
        P("exp", None),
        P("exp", None, SEQ),
        P("exp", None, SEQ),
        P("exp", SEQ, None),
        P("exp", None, SEQ),
        P("exp", None, SEQ),
    )
    return jax.shard_map(
        on_device, mesh=finer, in_specs=placed, out_specs=P(SEQ, "exp"), check_vma=False
    )
```

```python
import jax
import jax.numpy as jnp
from jax import lax
from jax.experimental import pallas as pl
from jax.experimental.pallas import tpu as pltpu
from jax.sharding import Mesh
from jax.sharding import PartitionSpec as P

D = 2880
HEAD_DIM = 64
WINDOW = 128
QH = 32
KVH = 4
TOPK = 4
EXPERTS = 32
CAP = 32
TOK = 128
BAND = 96
HALF = BAND // 2
COLS = D // 32
PART = 96
WIDE = D + TOK // 2
BLOCKS = 8
MINE = BLOCKS * CAP
EPSILON = 1e-05
SCALE = HEAD_DIM ** (-0.5)

BF = jnp.bfloat16
F32 = jnp.float32
SEQ = ("zh", "zl")


def dot(left, right, contract=((1,), (0,))):
    return lax.dot_general(left, right, (contract, ((), ())), preferred_element_type=F32)


def rows_of(shape):
    return lax.broadcasted_iota(jnp.int32, shape, 0)


def lanes_of(shape):
    return lax.broadcasted_iota(jnp.int32, shape, 1)


def split(value):
    high = value.astype(BF)
    return high, (value - high.astype(F32)).astype(BF)


def run(kernel, name, args, outs, scratch=(), room=16):
    def spec(shape):
        return pl.BlockSpec(shape, lambda i: (0,) * len(shape))

    scalars = pl.BlockSpec(memory_space=pltpu.SMEM)
    return pl.pallas_call(
        kernel,
        grid=(1,),
        in_specs=[scalars if a.dtype == jnp.int32 and a.ndim == 1 else spec(a.shape) for a in args],
        out_specs=[spec(shape) for shape, _ in outs],
        out_shape=[jax.ShapeDtypeStruct(shape, dtype) for shape, dtype in outs],
        scratch_shapes=list(scratch),
        compiler_params=pltpu.CompilerParams(vmem_limit_bytes=room * 1024 * 1024),
        name=name,
    )(*args)


def route_kernel(where, layer, gain, router, routes, adjoint, out_w, pay, inverse, shares, out_back):
    values = layer[...].astype(F32)
    inv = lax.rsqrt(jnp.sum(values * values, axis=0, keepdims=True) / D + EPSILON)
    inverse[...] = inv
    high, low = split(router[...].astype(F32) * gain[...].reshape(1, D))
    logits = (dot(high, layer[...]) + dot(low, layer[...])) * inv
    names = rows_of((EXPERTS, TOK))
    picked = [names == routes[k : k + 1, :] for k in range(TOPK)]
    raised = [
        jnp.exp(jnp.sum(jnp.where(p, logits, 0.0), axis=0, keepdims=True)) for p in picked
    ]
    total = raised[0] + raised[1] + raised[2] + raised[3]
    taken = sum(p.astype(F32) for p in picked)
    earlier = (rows_of((TOK, TOK)) < lanes_of((TOK, TOK))).astype(BF)
    ranks = dot(taken.astype(BF), earlier)
    line = rows_of((2 * TOPK, TOK))
    meta = jnp.zeros((2 * TOPK, TOK), F32)
    place = jnp.full((1, TOK), -1.0, F32)
    gate = jnp.zeros((1, TOK), F32)
    for k in range(TOPK):
        share = raised[k] / total
        shares[k : k + 1, :] = share
        rank = jnp.sum(jnp.where(picked[k], ranks, 0.0), axis=0, keepdims=True)
        name = routes[k : k + 1, :]
        meta = jnp.where(line == k, name.astype(F32), meta)
        meta = jnp.where(line == TOPK + k, rank, meta)
        place = jnp.where(name == where[0], rank, place)
        gate = jnp.where(name == where[0], share, gate)
    placing = jnp.where(rows_of((CAP, TOK)).astype(F32) == place, gate, 0.0).astype(BF)
    pay[:, 0:D] = dot(placing, adjoint[...], ((1,), (1,))).astype(BF)
    tail = jnp.concatenate(
        [meta[:, : TOK // 2], meta[:, TOK // 2 :], jnp.zeros((16, TOK // 2), F32)], axis=0
    )
    pay[:, D:] = tail.astype(BF)
    out_back[...] = dot(out_w[...], adjoint[...]).astype(BF)


def slots_kernel(metas, places):
    names = rows_of((EXPERTS, TOK)).astype(F32)
    for b in range(BLOCKS):
        tail = metas[b, :, :].astype(F32)
        meta = jnp.concatenate([tail[0 : 2 * TOPK, :], tail[2 * TOPK :, :]], axis=1)
        place = jnp.full((EXPERTS, TOK), -1.0, F32)
        for k in range(TOPK):
            match = names == meta[k : k + 1, :]
            place = jnp.where(match, meta[TOPK + k : TOPK + k + 1, :], place)
        places[:, b * TOK : (b + 1) * TOK] = place


def share_kernel(query_w, parts):
    for c in range(32):
        piece = query_w[:, c * COLS : (c + 1) * COLS]
        parts[c, :, :] = jnp.zeros((32, 256), BF)
        parts[c, :, 0:COLS] = piece[0:32]
        parts[c, :, 128 : 128 + COLS] = piece[32:64]


def pack_kernel(where, down, gate, up, store_g, store_u, to_next, to_prev, own_g, own_u):
    def chosen(parity):
        i, j = rows_of((16 * CAP, MINE)), lanes_of((16 * CAP, MINE))
        return (i == (2 * (j // CAP) + parity) * CAP + j % CAP).astype(BF)

    parity = where[1]
    here, there = chosen(parity), chosen(1 - parity)
    own_g[...] = dot(store_g[...], here).astype(BF)
    own_u[...] = dot(store_u[...], here).astype(BF)
    sent_g = dot(store_g[...], there).astype(BF)
    sent_u = dot(store_u[...], there).astype(BF)
    for first, ref in ((HALF, to_next), (0, to_prev)):
        for n, weight in enumerate((down, gate, up)):
            ref[n * HALF : (n + 1) * HALF, :] = weight[first : first + HALF, :]
        ref[3 * HALF :, :] = jnp.zeros((16, D), BF)
        for n, sent in enumerate((sent_g, sent_u)):
            for m in range(3):
                lane = (3 * n + m) * MINE
                ref[3 * HALF :, lane : lane + MINE] = sent[first + 16 * m : first + 16 * m + 16, :]


def attend_kernel(where, query, out_back, kv, kv_prev, next_q, aligned, grads):
    block = where[2]
    key_at, query_at = rows_of((TOK, TOK)), lanes_of((TOK, TOK))
    same = key_at <= query_at
    before = key_at > query_at

    def rows(q, out, before_kv, same_kv, before_mask):
        def half(kv_rows, mask):
            scores = dot(kv_rows[:, :HEAD_DIM], q) * SCALE
            return jnp.where(mask, jnp.exp(scores), 0.0), dot(kv_rows[:, HEAD_DIM:], out)

        p_before, a_before = half(before_kv, before_mask)
        p_same, a_same = half(same_kv, same)
        total = jnp.sum(p_before, axis=0, keepdims=True) + jnp.sum(p_same, axis=0, keepdims=True)
        p_before, p_same = p_before / total, p_same / total
        mean = jnp.sum(p_before * a_before, axis=0, keepdims=True) + jnp.sum(
            p_same * a_same, axis=0, keepdims=True
        )
        return (
            p_before.astype(BF),
            (p_before * (a_before - mean)).astype(BF),
            p_same.astype(BF),
            (p_same * (a_same - mean)).astype(BF),
        )

    q, out = query[...], out_back[...]
    own, prev, following = kv[...], kv_prev[...], next_q[TOK:, :]
    q_next, out_next = next_q[0:HEAD_DIM, :], next_q[HEAD_DIM : 2 * HEAD_DIM, :]
    _, sb_prev, p_own, sb_own = rows(q, out, prev, own, before & (block > 0))
    p_next, sb_next, _, _ = rows(q_next, out_next, own, following, before)
    live = jnp.where(block < 15, 1.0, 0.0)
    over = ((0,), (0,))
    across = ((1,), (1,))
    grads[0:64, :] = (
        (dot(prev[:, :HEAD_DIM], sb_prev, over) + dot(own[:, :HEAD_DIM], sb_own, over)) * SCALE
    ).astype(BF)
    grads[64:128, :] = (
        (dot(q, sb_own, across) + live * dot(q_next, sb_next, across)) * SCALE
    ).astype(BF)
    grads[128:192, :] = (dot(out, p_own, across) + live * dot(out_next, p_next, across)).astype(BF)
    line = rows_of((16, TOK))
    tail = jnp.zeros((16, TOK), F32)
    for k in range(TOPK):
        high = aligned[k : k + 1, :].astype(BF).astype(F32)
        tail = jnp.where(line == k, high, tail)
        tail = jnp.where(line == TOPK + k, aligned[k : k + 1, :] - high, tail)
    grads[192:208, :] = tail.astype(BF)


def expert_kernel(rows, down, gate, up, own_g, own_u, from_prev, from_next, sent, total):
    features = rows[:, :, 0:D].reshape(MINE, D)
    across = ((1,), (1,))

    def act(hidden, g, u):
        g, u = g.astype(F32), u.astype(F32)
        sigma = jax.nn.sigmoid(g)
        return (
            (hidden * u * (sigma * (1.0 + g * (1.0 - sigma)))).astype(BF),
            (hidden * (g * sigma)).astype(BF),
        )

    def stored(ref, n):
        return jnp.concatenate(
            [ref[3 * HALF :, (3 * n + m) * MINE : (3 * n + m + 1) * MINE] for m in range(3)], axis=0
        )

    backs = list(act(dot(down[...], features, across), own_g[...], own_u[...]))
    for ref in (from_prev, from_next):
        backs += list(act(dot(ref[0:HALF, :], features, across), stored(ref, 0), stored(ref, 1)))
    weights = [gate[...], up[...]]
    for ref in (from_prev, from_next):
        weights += [ref[HALF : 2 * HALF, :], ref[2 * HALF : 3 * HALF, :]]
    total[0:D, :] = dot(
        jnp.concatenate(weights, axis=0), jnp.concatenate(backs, axis=0), ((0,), (0,))
    )
    total[D:, :] = jnp.zeros((8, MINE), F32)
    for c in range(32):
        sent[c, :, :] = total[c * COLS : c * COLS + PART, :].astype(BF)


def combine_kernel(returned, places, sent):
    slot = rows_of((CAP, TOK)).astype(F32)
    empty = jnp.zeros((CAP, TOK), BF)
    for h in range(2):
        total = jnp.zeros((PART, 4 * TOK), F32)
        for pair in range(0, EXPERTS, 2):
            picks = []
            for e in (pair, pair + 1):
                for b in range(4):
                    lanes = slice((4 * h + b) * TOK, (4 * h + b + 1) * TOK)
                    pick = (slot == places[e : e + 1, lanes]).astype(BF)
                    picks.append(jnp.concatenate([empty] * b + [pick] + [empty] * (3 - b), axis=1))
            terms = [returned[e, :, h * TOK : (h + 1) * TOK] for e in (pair, pair + 1)]
            total = total + dot(jnp.concatenate(terms, axis=1), jnp.concatenate(picks, axis=0))
        for b in range(4):
            sent[4 * h + b, :, :] = total[:, b * TOK : (b + 1) * TOK].astype(BF)


def project_kernel(grads, rows, key_w, value_w, router, shares, routes, attended):
    total = jnp.zeros((PART, TOK), F32)
    for h in range(QH):
        for n in range(2):
            weight = rows[h, :, n * 128 : n * 128 + PART]
            total = total + dot(weight, grads[h, 32 * n : 32 * n + 32, :], ((0,), (0,)))
    group = QH // KVH
    for first, weight in ((64, key_w), (128, value_w)):
        sums = []
        for g in range(KVH):
            some = grads[g * group, first : first + 64, :].astype(F32)
            for h in range(g * group + 1, (g + 1) * group):
                some = some + grads[h, first : first + 64, :].astype(F32)
            sums.append(some)
        high, low = split(jnp.concatenate(sums, axis=0))
        total = total + dot(weight[...], high) + dot(weight[...], low)
    tail = grads[0, 192:208, :].astype(F32)
    for h in range(1, QH):
        tail = tail + grads[h, 192:208, :].astype(F32)
    aligned = [tail[k : k + 1, :] + tail[TOPK + k : TOPK + k + 1, :] for k in range(TOPK)]
    mean = sum(shares[k : k + 1, :] * aligned[k] for k in range(TOPK))
    names = rows_of((EXPERTS, TOK))
    coef = jnp.zeros((EXPERTS, TOK), F32)
    for k in range(TOPK):
        back = shares[k : k + 1, :] * (aligned[k] - mean)
        coef = jnp.where(names == routes[k : k + 1, :], back, coef)
    high, low = split(coef)
    attended[...] = total + dot(router[...], high) + dot(router[...], low)


def lift_kernel(bands, attended, gain, values, lifted, stat):
    total = attended[...]
    for b in range(BLOCKS):
        total = total + bands[b, :, :].astype(F32)
    total = jnp.where(rows_of((PART, TOK)) < COLS, total, 0.0) * gain[...]
    lifted[...] = total
    stat[...] = jnp.broadcast_to(
        jnp.sum(values[...] * total, axis=0, keepdims=True), (32, TOK)
    )


def finish_kernel(stats, lifted, values, inverse, base, result):
    mean = jnp.sum(stats[...], axis=0, keepdims=True) / D
    inv = inverse[...]
    result[...] = base[...] + (
        inv * lifted[0:COLS, :] - values[0:COLS, :] * (inv * inv * inv * mean)
    )


def on_device(
    adjoint,
    seed_grad,
    layer_input,
    norm_gain,
    router_weight,
    routes,
    expert_out,
    stored_query,
    stored_key,
    stored_value,
    query_weight,
    key_weight,
    value_weight,
    output_weight,
    gate_weight,
    up_weight,
    down_weight,
    stored_gate,
    stored_up,
):
    col = lax.axis_index("exp")
    block = lax.axis_index(SEQ)
    parity = lax.axis_index("zl")
    where = jnp.stack([col, parity, block]).astype(jnp.int32)
    first = col * COLS
    adjoint_t, layer_t, routes_t, router_t = adjoint.T, layer_input.T, routes.T, router_weight.T
    to_next = [(i, (i + 1) % 16) for i in range(16)]
    to_prev = [(j, i) for i, j in to_next]

    pay, inverse, shares, out_back = run(
        route_kernel,
        "route",
        (where, layer_t, norm_gain, router_t, routes_t, adjoint_t, output_weight),
        [((CAP, WIDE), BF), ((1, TOK), F32), ((TOPK, TOK), F32), ((HEAD_DIM, TOK), BF)],
        room=60,
    )
    gathered = lax.all_gather(pay, "zh", axis=0)

    down, gate, up = down_weight[0], gate_weight[0].T, up_weight[0].T
    wide, narrow = ((3 * HALF + 16, D), BF), ((BAND, MINE), BF)
    w_next, w_prev, own_g, own_u = run(
        pack_kernel,
        "pack",
        (where, down, gate, up, stored_gate[0].T, stored_up[0].T),
        [wide, wide, narrow, narrow],
    )

    w_next, w_prev, query_weight = lax.optimization_barrier((w_next, w_prev, query_weight))
    w_from_prev = lax.ppermute(w_next, SEQ, to_next)
    w_from_next = lax.ppermute(w_prev, SEQ, to_prev)

    (query_parts,) = run(share_kernel, "share", (query_weight.T,), [((32, 32, 256), BF)])
    query_cols = lax.all_to_all(query_parts, "exp", 0, 0, tiled=True)
    kv_start = col // (QH // KVH) * HEAD_DIM
    kv = jnp.concatenate(
        [lax.dynamic_slice_in_dim(a, kv_start, HEAD_DIM, 1) for a in (stored_key, stored_value)], axis=1
    )
    query_t = stored_query.T
    kv_prev = lax.ppermute(kv, SEQ, to_next)
    from_next_q = lax.ppermute(jnp.concatenate([query_t, out_back, kv], axis=0), SEQ, to_prev)
    kv_prev, from_next_q, w_from_prev, w_from_next = lax.optimization_barrier(
        (kv_prev, from_next_q, w_from_prev, w_from_next)
    )
    adjoint_cols = lax.dynamic_slice_in_dim(adjoint_t, first, COLS, 0).astype(F32)
    values = lax.dynamic_slice_in_dim(layer_t, first, COLS, 0).astype(F32)
    aligned = jnp.sum(adjoint_cols[:, None, :] * expert_out.transpose(2, 1, 0).astype(F32), axis=0)
    (grads,) = run(
        attend_kernel,
        "attend",
        (where, query_t, out_back, kv, kv_prev, from_next_q, aligned),
        [((208, TOK), BF)],
    )
    gathered, grads, query_cols = lax.optimization_barrier((gathered, grads, query_cols))
    all_grads = lax.all_gather(grads, "exp", axis=0)
    (terms,) = run(
        expert_kernel,
        "expert",
        (gathered, down, gate, up, own_g, own_u, w_from_prev, w_from_next),
        [((32, PART, MINE), BF)],
        [pltpu.VMEM((D + 8, MINE), F32)],
        room=32,
    )
    returned = lax.all_to_all(terms, "exp", 0, 0, tiled=True)
    (places,) = run(
        slots_kernel, "slots", (gathered[:, 0:16, D:],), [((EXPERTS, BLOCKS * TOK), F32)]
    )
    (sums,) = run(combine_kernel, "combine", (returned, places), [((BLOCKS, PART, TOK), BF)])
    bands = lax.all_to_all(sums, "zh", 0, 0, tiled=True)

    pad = ((0, PART - COLS), (0, 0))
    router_cols = jnp.pad(lax.dynamic_slice_in_dim(router_weight, first, COLS, 0), pad)
    (attended,) = run(
        project_kernel,
        "project",
        (all_grads, query_cols, jnp.pad(key_weight, pad), jnp.pad(value_weight, pad), router_cols, shares, routes_t),
        [((PART, TOK), F32)],
    )
    gain = jnp.pad(lax.dynamic_slice_in_dim(norm_gain, first, COLS, 0)[:, None], pad)
    values = jnp.pad(values, pad)
    lifted, stat = run(
        lift_kernel, "lift", (bands, attended, gain, values), [((PART, TOK), F32), ((32, TOK), F32)]
    )
    stats = lax.all_to_all(stat, "exp", 0, 0, tiled=True)
    (result,) = run(
        finish_kernel,
        "finish",
        (stats, lifted, values, inverse, seed_grad.T + adjoint_cols),
        [((COLS, TOK), F32)],
    )
    return result.T


def solution(mesh):
    finer = Mesh(mesh.devices.reshape(8, 2, 32), ("zh", "zl", "exp"))
    placed = (
        P(SEQ, None),
        P(SEQ, "exp"),
        P(SEQ, None),
        P(),
        P(),
        P(SEQ, None),
        P(SEQ, None, "exp"),
        P(SEQ, "exp"),
        P(SEQ, None),
        P(SEQ, None),
        P(None, "exp"),
        P("exp", None),
        P("exp", None),
        P("exp", None),
        P("exp", None, SEQ),
        P("exp", None, SEQ),
        P("exp", SEQ, None),
        P("exp", None, SEQ),
        P("exp", None, SEQ),
    )
    return jax.shard_map(
        on_device, mesh=finer, in_specs=placed, out_specs=P(SEQ, "exp"), check_vma=False
    )
```

```python
import jax
import jax.numpy as jnp
from jax import lax
from jax.experimental import pallas as pl
from jax.experimental.pallas import tpu as pltpu
from jax.sharding import Mesh
from jax.sharding import PartitionSpec as P

D = 2880
HEAD_DIM = 64
WINDOW = 128
QH = 32
KVH = 4
TOPK = 4
EXPERTS = 32
CAP = 32
TOK = 128
BAND = 96
HALF = BAND // 2
COLS = D // 32
PART = 96
WIDE = D + TOK // 2
BLOCKS = 8
MINE = BLOCKS * CAP
EPSILON = 1e-05
SCALE = HEAD_DIM ** (-0.5)

BF = jnp.bfloat16
F32 = jnp.float32
SEQ = ("zh", "zl")


def dot(left, right, contract=((1,), (0,))):
    return lax.dot_general(left, right, (contract, ((), ())), preferred_element_type=F32)


def rows_of(shape):
    return lax.broadcasted_iota(jnp.int32, shape, 0)


def lanes_of(shape):
    return lax.broadcasted_iota(jnp.int32, shape, 1)


def split(value):
    high = value.astype(BF)
    return high, (value - high.astype(F32)).astype(BF)


def run(kernel, name, args, outs, scratch=(), room=16):
    def spec(shape):
        return pl.BlockSpec(shape, lambda i: (0,) * len(shape))

    scalars = pl.BlockSpec(memory_space=pltpu.SMEM)
    return pl.pallas_call(
        kernel,
        grid=(1,),
        in_specs=[scalars if a.dtype == jnp.int32 and a.ndim == 1 else spec(a.shape) for a in args],
        out_specs=[spec(shape) for shape, _ in outs],
        out_shape=[jax.ShapeDtypeStruct(shape, dtype) for shape, dtype in outs],
        scratch_shapes=list(scratch),
        compiler_params=pltpu.CompilerParams(vmem_limit_bytes=room * 1024 * 1024),
        name=name,
    )(*args)


def route_kernel(where, layer, gain, router, routes, adjoint, out_w, pay, inverse, shares, out_back):
    values = layer[...].astype(F32)
    inv = lax.rsqrt(jnp.sum(values * values, axis=0, keepdims=True) / D + EPSILON)
    inverse[...] = inv
    high, low = split(router[...].astype(F32) * gain[...].reshape(1, D))
    logits = (dot(high, layer[...]) + dot(low, layer[...])) * inv
    names = rows_of((EXPERTS, TOK))
    picked = [names == routes[k : k + 1, :] for k in range(TOPK)]
    raised = [
        jnp.exp(jnp.sum(jnp.where(p, logits, 0.0), axis=0, keepdims=True)) for p in picked
    ]
    total = raised[0] + raised[1] + raised[2] + raised[3]
    taken = sum(p.astype(F32) for p in picked)
    earlier = (rows_of((TOK, TOK)) < lanes_of((TOK, TOK))).astype(BF)
    ranks = dot(taken.astype(BF), earlier)
    line = rows_of((2 * TOPK, TOK))
    meta = jnp.zeros((2 * TOPK, TOK), F32)
    place = jnp.full((1, TOK), -1.0, F32)
    gate = jnp.zeros((1, TOK), F32)
    for k in range(TOPK):
        share = raised[k] / total
        shares[k : k + 1, :] = share
        rank = jnp.sum(jnp.where(picked[k], ranks, 0.0), axis=0, keepdims=True)
        name = routes[k : k + 1, :]
        meta = jnp.where(line == k, name.astype(F32), meta)
        meta = jnp.where(line == TOPK + k, rank, meta)
        place = jnp.where(name == where[0], rank, place)
        gate = jnp.where(name == where[0], share, gate)
    placing = jnp.where(rows_of((CAP, TOK)).astype(F32) == place, gate, 0.0).astype(BF)
    pay[:, 0:D] = dot(placing, adjoint[...], ((1,), (1,))).astype(BF)
    tail = jnp.concatenate(
        [meta[:, : TOK // 2], meta[:, TOK // 2 :], jnp.zeros((16, TOK // 2), F32)], axis=0
    )
    pay[:, D:] = tail.astype(BF)
    out_back[...] = dot(out_w[...], adjoint[...]).astype(BF)


def slots_kernel(metas, places):
    names = rows_of((EXPERTS, TOK)).astype(F32)
    for b in range(BLOCKS):
        tail = metas[b, :, :].astype(F32)
        meta = jnp.concatenate([tail[0 : 2 * TOPK, :], tail[2 * TOPK :, :]], axis=1)
        place = jnp.full((EXPERTS, TOK), -1.0, F32)
        for k in range(TOPK):
            match = names == meta[k : k + 1, :]
            place = jnp.where(match, meta[TOPK + k : TOPK + k + 1, :], place)
        places[:, b * TOK : (b + 1) * TOK] = place


def share_kernel(query_w, parts):
    for c in range(32):
        piece = query_w[:, c * COLS : (c + 1) * COLS]
        parts[c, :, :] = jnp.zeros((32, 256), BF)
        parts[c, :, 0:COLS] = piece[0:32]
        parts[c, :, 128 : 128 + COLS] = piece[32:64]


def pack_kernel(where, down, gate, up, store_g, store_u, to_next, to_prev, own_g, own_u):
    def chosen(parity):
        i, j = rows_of((16 * CAP, MINE)), lanes_of((16 * CAP, MINE))
        return (i == (2 * (j // CAP) + parity) * CAP + j % CAP).astype(BF)

    parity = where[1]
    here, there = chosen(parity), chosen(1 - parity)
    own_g[...] = dot(store_g[...], here).astype(BF)
    own_u[...] = dot(store_u[...], here).astype(BF)
    sent_g = dot(store_g[...], there).astype(BF)
    sent_u = dot(store_u[...], there).astype(BF)
    for first, ref in ((HALF, to_next), (0, to_prev)):
        for n, weight in enumerate((down, gate, up)):
            ref[n * HALF : (n + 1) * HALF, :] = weight[first : first + HALF, :]
        ref[3 * HALF :, :] = jnp.zeros((16, D), BF)
        for n, sent in enumerate((sent_g, sent_u)):
            for m in range(3):
                lane = (3 * n + m) * MINE
                ref[3 * HALF :, lane : lane + MINE] = sent[first + 16 * m : first + 16 * m + 16, :]


def attend_kernel(where, query, out_back, kv, kv_prev, next_q, grads):
    block = where[2]
    key_at, query_at = rows_of((TOK, TOK)), lanes_of((TOK, TOK))
    same = key_at <= query_at
    before = key_at > query_at

    def rows(q, out, before_kv, same_kv, before_mask):
        def half(kv_rows, mask):
            scores = dot(kv_rows[:, :HEAD_DIM], q) * SCALE
            return jnp.where(mask, jnp.exp(scores), 0.0), dot(kv_rows[:, HEAD_DIM:], out)

        p_before, a_before = half(before_kv, before_mask)
        p_same, a_same = half(same_kv, same)
        total = jnp.sum(p_before, axis=0, keepdims=True) + jnp.sum(p_same, axis=0, keepdims=True)
        p_before, p_same = p_before / total, p_same / total
        mean = jnp.sum(p_before * a_before, axis=0, keepdims=True) + jnp.sum(
            p_same * a_same, axis=0, keepdims=True
        )
        return (
            p_before.astype(BF),
            (p_before * (a_before - mean)).astype(BF),
            p_same.astype(BF),
            (p_same * (a_same - mean)).astype(BF),
        )

    q, out = query[...], out_back[...]
    own, prev, following = kv[...], kv_prev[...], next_q[TOK:, :]
    q_next, out_next = next_q[0:HEAD_DIM, :], next_q[HEAD_DIM : 2 * HEAD_DIM, :]
    _, sb_prev, p_own, sb_own = rows(q, out, prev, own, before & (block > 0))
    p_next, sb_next, _, _ = rows(q_next, out_next, own, following, before)
    live = jnp.where(block < 15, 1.0, 0.0)
    over = ((0,), (0,))
    across = ((1,), (1,))
    grads[0:64, :] = (
        (dot(prev[:, :HEAD_DIM], sb_prev, over) + dot(own[:, :HEAD_DIM], sb_own, over)) * SCALE
    ).astype(BF)
    grads[64:128, :] = (
        (dot(q, sb_own, across) + live * dot(q_next, sb_next, across)) * SCALE
    ).astype(BF)
    grads[128:192, :] = (dot(out, p_own, across) + live * dot(out_next, p_next, across)).astype(BF)


def expert_kernel(rows, down, gate, up, own_g, own_u, from_prev, from_next, aligned, sent, total):
    features = rows[:, :, 0:D].reshape(MINE, D)
    across = ((1,), (1,))

    def act(hidden, g, u):
        g, u = g.astype(F32), u.astype(F32)
        sigma = jax.nn.sigmoid(g)
        return (
            (hidden * u * (sigma * (1.0 + g * (1.0 - sigma)))).astype(BF),
            (hidden * (g * sigma)).astype(BF),
        )

    def stored(ref, n):
        return jnp.concatenate(
            [ref[3 * HALF :, (3 * n + m) * MINE : (3 * n + m + 1) * MINE] for m in range(3)], axis=0
        )

    backs = list(act(dot(down[...], features, across), own_g[...], own_u[...]))
    for ref in (from_prev, from_next):
        backs += list(act(dot(ref[0:HALF, :], features, across), stored(ref, 0), stored(ref, 1)))
    weights = [gate[...], up[...]]
    for ref in (from_prev, from_next):
        weights += [ref[HALF : 2 * HALF, :], ref[2 * HALF : 3 * HALF, :]]
    total[0:D, :] = dot(
        jnp.concatenate(weights, axis=0), jnp.concatenate(backs, axis=0), ((0,), (0,))
    )
    total[D:, :] = jnp.zeros((8, MINE), F32)
    line = rows_of((PART, MINE))
    tail = jnp.zeros((PART, MINE), F32)
    for k in range(TOPK):
        value = aligned[k : k + 1, :]
        high = value.astype(BF).astype(F32)
        tail = jnp.where(line == COLS + k, jnp.concatenate([high, value - high], axis=1), tail)
    for c in range(32):
        sent[c, :, :] = jnp.where(line < COLS, total[c * COLS : c * COLS + PART, :], tail).astype(BF)


def combine_kernel(returned, places, sent, aligned):
    slot = rows_of((CAP, TOK)).astype(F32)
    empty = jnp.zeros((CAP, TOK), BF)
    for h in range(2):
        total = jnp.zeros((PART, 4 * TOK), F32)
        for pair in range(0, EXPERTS, 2):
            picks = []
            for e in (pair, pair + 1):
                for b in range(4):
                    lanes = slice((4 * h + b) * TOK, (4 * h + b + 1) * TOK)
                    pick = (slot == places[e : e + 1, lanes]).astype(BF)
                    picks.append(jnp.concatenate([empty] * b + [pick] + [empty] * (3 - b), axis=1))
            terms = [returned[e, :, h * TOK : (h + 1) * TOK] for e in (pair, pair + 1)]
            total = total + dot(jnp.concatenate(terms, axis=1), jnp.concatenate(picks, axis=0))
        for b in range(4):
            sent[4 * h + b, :, :] = total[:, b * TOK : (b + 1) * TOK].astype(BF)
    tail = jnp.zeros((16, MINE), F32)
    for e in range(EXPERTS):
        tail = tail + returned[e, PART - 16 :, :].astype(F32)
    first = COLS - (PART - 16)
    aligned[...] = tail[first : first + TOPK, 0:TOK] + tail[first : first + TOPK, TOK:]


def project_kernel(grads, rows, key_w, value_w, router, shares, routes, sums, attended):
    total = jnp.zeros((PART, TOK), F32)
    for h in range(QH):
        for n in range(2):
            weight = rows[h, :, n * 128 : n * 128 + PART]
            total = total + dot(weight, grads[h, 32 * n : 32 * n + 32, :], ((0,), (0,)))
    group = QH // KVH
    for first, weight in ((64, key_w), (128, value_w)):
        groups = []
        for g in range(KVH):
            some = grads[g * group, first : first + 64, :].astype(F32)
            for h in range(g * group + 1, (g + 1) * group):
                some = some + grads[h, first : first + 64, :].astype(F32)
            groups.append(some)
        high, low = split(jnp.concatenate(groups, axis=0))
        total = total + dot(weight[...], high) + dot(weight[...], low)
    aligned = [sums[k : k + 1, :] for k in range(TOPK)]
    mean = sum(shares[k : k + 1, :] * aligned[k] for k in range(TOPK))
    names = rows_of((EXPERTS, TOK))
    coef = jnp.zeros((EXPERTS, TOK), F32)
    for k in range(TOPK):
        back = shares[k : k + 1, :] * (aligned[k] - mean)
        coef = jnp.where(names == routes[k : k + 1, :], back, coef)
    high, low = split(coef)
    attended[...] = total + dot(router[...], high) + dot(router[...], low)


def lift_kernel(bands, attended, gain, values, lifted, stat):
    total = attended[...]
    for b in range(BLOCKS):
        total = total + bands[b, :, :].astype(F32)
    total = jnp.where(rows_of((PART, TOK)) < COLS, total, 0.0) * gain[...]
    lifted[...] = total
    stat[...] = jnp.broadcast_to(
        jnp.sum(values[...] * total, axis=0, keepdims=True), (32, TOK)
    )


def finish_kernel(stats, lifted, values, inverse, base, result):
    mean = jnp.sum(stats[...], axis=0, keepdims=True) / D
    inv = inverse[...]
    result[...] = base[...] + (
        inv * lifted[0:COLS, :] - values[0:COLS, :] * (inv * inv * inv * mean)
    )


def on_device(
    adjoint,
    seed_grad,
    layer_input,
    norm_gain,
    router_weight,
    routes,
    expert_out,
    stored_query,
    stored_key,
    stored_value,
    query_weight,
    key_weight,
    value_weight,
    output_weight,
    gate_weight,
    up_weight,
    down_weight,
    stored_gate,
    stored_up,
):
    col = lax.axis_index("exp")
    block = lax.axis_index(SEQ)
    parity = lax.axis_index("zl")
    where = jnp.stack([col, parity, block]).astype(jnp.int32)
    first = col * COLS
    adjoint_t, layer_t, routes_t, router_t = adjoint.T, layer_input.T, routes.T, router_weight.T
    to_next = [(i, (i + 1) % 16) for i in range(16)]
    to_prev = [(j, i) for i, j in to_next]

    pay, inverse, shares, out_back = run(
        route_kernel,
        "route",
        (where, layer_t, norm_gain, router_t, routes_t, adjoint_t, output_weight),
        [((CAP, WIDE), BF), ((1, TOK), F32), ((TOPK, TOK), F32), ((HEAD_DIM, TOK), BF)],
        room=60,
    )
    gathered = lax.all_gather(pay, "zh", axis=0)

    down, gate, up = down_weight[0], gate_weight[0].T, up_weight[0].T
    wide, narrow = ((3 * HALF + 16, D), BF), ((BAND, MINE), BF)
    w_next, w_prev, own_g, own_u = run(
        pack_kernel,
        "pack",
        (where, down, gate, up, stored_gate[0].T, stored_up[0].T),
        [wide, wide, narrow, narrow],
    )

    w_next, w_prev, query_weight = lax.optimization_barrier((w_next, w_prev, query_weight))
    w_from_prev = lax.ppermute(w_next, SEQ, to_next)
    w_from_next = lax.ppermute(w_prev, SEQ, to_prev)

    (query_parts,) = run(share_kernel, "share", (query_weight.T,), [((32, 32, 256), BF)])
    query_cols = lax.all_to_all(query_parts, "exp", 0, 0, tiled=True)
    kv_start = col // (QH // KVH) * HEAD_DIM
    kv = jnp.concatenate(
        [lax.dynamic_slice_in_dim(a, kv_start, HEAD_DIM, 1) for a in (stored_key, stored_value)], axis=1
    )
    query_t = stored_query.T
    kv_prev = lax.ppermute(kv, SEQ, to_next)
    from_next_q = lax.ppermute(jnp.concatenate([query_t, out_back, kv], axis=0), SEQ, to_prev)
    adjoint_cols = lax.dynamic_slice_in_dim(adjoint_t, first, COLS, 0).astype(F32)
    values = lax.dynamic_slice_in_dim(layer_t, first, COLS, 0).astype(F32)
    aligned = jnp.sum(adjoint_cols[:, None, :] * expert_out.transpose(2, 1, 0).astype(F32), axis=0)
    kv_prev, from_next_q, w_from_prev, w_from_next, aligned = lax.optimization_barrier(
        (kv_prev, from_next_q, w_from_prev, w_from_next, aligned)
    )
    (grads,) = run(
        attend_kernel,
        "attend",
        (where, query_t, out_back, kv, kv_prev, from_next_q),
        [((192, TOK), BF)],
    )
    gathered, grads, query_cols = lax.optimization_barrier((gathered, grads, query_cols))
    all_grads = lax.all_gather(grads, "exp", axis=0)
    (terms,) = run(
        expert_kernel,
        "expert",
        (gathered, down, gate, up, own_g, own_u, w_from_prev, w_from_next, aligned),
        [((32, PART, MINE), BF)],
        [pltpu.VMEM((D + 8, MINE), F32)],
        room=32,
    )
    returned = lax.all_to_all(terms, "exp", 0, 0, tiled=True)
    (places,) = run(
        slots_kernel, "slots", (gathered[:, 0:16, D:],), [((EXPERTS, BLOCKS * TOK), F32)]
    )
    sums, aligned_sums = run(
        combine_kernel,
        "combine",
        (returned, places),
        [((BLOCKS, PART, TOK), BF), ((TOPK, TOK), F32)],
    )
    bands = lax.all_to_all(sums, "zh", 0, 0, tiled=True)

    pad = ((0, PART - COLS), (0, 0))
    router_cols = jnp.pad(lax.dynamic_slice_in_dim(router_weight, first, COLS, 0), pad)
    (attended,) = run(
        project_kernel,
        "project",
        (all_grads, query_cols, jnp.pad(key_weight, pad), jnp.pad(value_weight, pad), router_cols, shares, routes_t, aligned_sums),
        [((PART, TOK), F32)],
    )
    gain = jnp.pad(lax.dynamic_slice_in_dim(norm_gain, first, COLS, 0)[:, None], pad)
    values = jnp.pad(values, pad)
    lifted, stat = run(
        lift_kernel, "lift", (bands, attended, gain, values), [((PART, TOK), F32), ((32, TOK), F32)]
    )
    stats = lax.all_to_all(stat, "exp", 0, 0, tiled=True)
    (result,) = run(
        finish_kernel,
        "finish",
        (stats, lifted, values, inverse, seed_grad.T + adjoint_cols),
        [((COLS, TOK), F32)],
    )
    return result.T


def solution(mesh):
    finer = Mesh(mesh.devices.reshape(8, 2, 32), ("zh", "zl", "exp"))
    placed = (
        P(SEQ, None),
        P(SEQ, "exp"),
        P(SEQ, None),
        P(),
        P(),
        P(SEQ, None),
        P(SEQ, None, "exp"),
        P(SEQ, "exp"),
        P(SEQ, None),
        P(SEQ, None),
        P(None, "exp"),
        P("exp", None),
        P("exp", None),
        P("exp", None),
        P("exp", None, SEQ),
        P("exp", None, SEQ),
        P("exp", SEQ, None),
        P("exp", None, SEQ),
        P("exp", None, SEQ),
    )
    return jax.shard_map(
        on_device, mesh=finer, in_specs=placed, out_specs=P(SEQ, "exp"), check_vma=False
    )
```

```python
import jax
import jax.numpy as jnp
from jax import lax
from jax.experimental import pallas as pl
from jax.experimental.pallas import tpu as pltpu
from jax.sharding import Mesh
from jax.sharding import PartitionSpec as P

D = 2880
HEAD_DIM = 64
WINDOW = 128
QH = 32
KVH = 4
TOPK = 4
EXPERTS = 32
CAP = 32
TOK = 128
BAND = 96
HALF = BAND // 2
COLS = D // 32
PART = 96
WIDE = D + TOK // 2
BLOCKS = 8
MINE = BLOCKS * CAP
EPSILON = 1e-05
SCALE = HEAD_DIM ** (-0.5)

BF = jnp.bfloat16
F32 = jnp.float32
SEQ = ("zh", "zl")


def dot(left, right, contract=((1,), (0,))):
    return lax.dot_general(left, right, (contract, ((), ())), preferred_element_type=F32)


def rows_of(shape):
    return lax.broadcasted_iota(jnp.int32, shape, 0)


def lanes_of(shape):
    return lax.broadcasted_iota(jnp.int32, shape, 1)


def split(value):
    high = value.astype(BF)
    return high, (value - high.astype(F32)).astype(BF)


def run(kernel, name, args, outs, scratch=(), room=16):
    def spec(shape):
        return pl.BlockSpec(shape, lambda i: (0,) * len(shape))

    scalars = pl.BlockSpec(memory_space=pltpu.SMEM)
    return pl.pallas_call(
        kernel,
        grid=(1,),
        in_specs=[scalars if a.dtype == jnp.int32 and a.ndim == 1 else spec(a.shape) for a in args],
        out_specs=[spec(shape) for shape, _ in outs],
        out_shape=[jax.ShapeDtypeStruct(shape, dtype) for shape, dtype in outs],
        scratch_shapes=list(scratch),
        compiler_params=pltpu.CompilerParams(vmem_limit_bytes=room * 1024 * 1024),
        name=name,
    )(*args)


def route_kernel(where, layer, gain, router, routes, adjoint, out_w, pay, inverse, shares, out_back):
    values = layer[...].astype(F32)
    inv = lax.rsqrt(jnp.sum(values * values, axis=0, keepdims=True) / D + EPSILON)
    inverse[...] = inv
    high, low = split(router[...].astype(F32) * gain[...].reshape(1, D))
    both = dot(jnp.concatenate([high, low], axis=0), layer[...])
    logits = (both[0:EXPERTS] + both[EXPERTS:]) * inv
    names = rows_of((EXPERTS, TOK))
    picked = [names == routes[k : k + 1, :] for k in range(TOPK)]
    raised = [
        jnp.exp(jnp.sum(jnp.where(p, logits, 0.0), axis=0, keepdims=True)) for p in picked
    ]
    total = raised[0] + raised[1] + raised[2] + raised[3]
    taken = sum(p.astype(F32) for p in picked)
    earlier = (rows_of((TOK, TOK)) < lanes_of((TOK, TOK))).astype(BF)
    ranks = dot(taken.astype(BF), earlier)
    line = rows_of((2 * TOPK, TOK))
    meta = jnp.zeros((2 * TOPK, TOK), F32)
    place = jnp.full((1, TOK), -1.0, F32)
    gate = jnp.zeros((1, TOK), F32)
    for k in range(TOPK):
        share = raised[k] / total
        shares[k : k + 1, :] = share
        rank = jnp.sum(jnp.where(picked[k], ranks, 0.0), axis=0, keepdims=True)
        name = routes[k : k + 1, :]
        meta = jnp.where(line == k, name.astype(F32), meta)
        meta = jnp.where(line == TOPK + k, rank, meta)
        place = jnp.where(name == where[0], rank, place)
        gate = jnp.where(name == where[0], share, gate)
    placing = jnp.where(rows_of((CAP, TOK)).astype(F32) == place, gate, 0.0).astype(BF)
    pay[:, 0:D] = dot(placing, adjoint[...], ((1,), (1,))).astype(BF)
    tail = jnp.concatenate(
        [meta[:, : TOK // 2], meta[:, TOK // 2 :], jnp.zeros((16, TOK // 2), F32)], axis=0
    )
    pay[:, D:] = tail.astype(BF)
    out_back[...] = dot(out_w[...], adjoint[...]).astype(BF)


def slots_kernel(metas, places):
    names = rows_of((EXPERTS, TOK)).astype(F32)
    for b in range(BLOCKS):
        tail = metas[b, :, :].astype(F32)
        meta = jnp.concatenate([tail[0 : 2 * TOPK, :], tail[2 * TOPK :, :]], axis=1)
        place = jnp.full((EXPERTS, TOK), -1.0, F32)
        for k in range(TOPK):
            match = names == meta[k : k + 1, :]
            place = jnp.where(match, meta[TOPK + k : TOPK + k + 1, :], place)
        places[:, b * TOK : (b + 1) * TOK] = place


def share_kernel(query_w, parts):
    for c in range(32):
        piece = query_w[:, c * COLS : (c + 1) * COLS]
        parts[c, :, :] = jnp.zeros((32, 256), BF)
        parts[c, :, 0:COLS] = piece[0:32]
        parts[c, :, 128 : 128 + COLS] = piece[32:64]


def pack_kernel(where, down, gate, up, store_g, store_u, to_next, to_prev, own_g, own_u):
    def chosen(parity):
        i, j = rows_of((16 * CAP, MINE)), lanes_of((16 * CAP, MINE))
        return (i == (2 * (j // CAP) + parity) * CAP + j % CAP).astype(BF)

    parity = where[1]
    here, there = chosen(parity), chosen(1 - parity)
    own_g[...] = dot(store_g[...], here).astype(BF)
    own_u[...] = dot(store_u[...], here).astype(BF)
    sent_g = dot(store_g[...], there).astype(BF)
    sent_u = dot(store_u[...], there).astype(BF)
    for first, ref in ((HALF, to_next), (0, to_prev)):
        for n, weight in enumerate((down, gate, up)):
            ref[n * HALF : (n + 1) * HALF, :] = weight[first : first + HALF, :]
        ref[3 * HALF :, :] = jnp.zeros((16, D), BF)
        for n, sent in enumerate((sent_g, sent_u)):
            for m in range(3):
                lane = (3 * n + m) * MINE
                ref[3 * HALF :, lane : lane + MINE] = sent[first + 16 * m : first + 16 * m + 16, :]


def attend_kernel(where, query, out_back, kv, kv_prev, next_q, aligned, grads):
    block = where[2]
    key_at, query_at = rows_of((TOK, TOK)), lanes_of((TOK, TOK))
    same = key_at <= query_at
    before = key_at > query_at

    def rows(q, out, before_kv, same_kv, before_mask):
        def half(kv_rows, mask):
            scores = dot(kv_rows[:, :HEAD_DIM], q) * SCALE
            return jnp.where(mask, jnp.exp(scores), 0.0), dot(kv_rows[:, HEAD_DIM:], out)

        p_before, a_before = half(before_kv, before_mask)
        p_same, a_same = half(same_kv, same)
        total = jnp.sum(p_before, axis=0, keepdims=True) + jnp.sum(p_same, axis=0, keepdims=True)
        p_before, p_same = p_before / total, p_same / total
        mean = jnp.sum(p_before * a_before, axis=0, keepdims=True) + jnp.sum(
            p_same * a_same, axis=0, keepdims=True
        )
        return (
            p_before.astype(BF),
            (p_before * (a_before - mean)).astype(BF),
            p_same.astype(BF),
            (p_same * (a_same - mean)).astype(BF),
        )

    q, out = query[...], out_back[...]
    own, prev, following = kv[...], kv_prev[...], next_q[TOK:, :]
    q_next, out_next = next_q[0:HEAD_DIM, :], next_q[HEAD_DIM : 2 * HEAD_DIM, :]
    _, sb_prev, p_own, sb_own = rows(q, out, prev, own, before & (block > 0))
    p_next, sb_next, _, _ = rows(q_next, out_next, own, following, before)
    live = jnp.where(block < 15, 1.0, 0.0)
    over = ((0,), (0,))
    across = ((1,), (1,))
    grads[0:64, :] = (
        (dot(prev[:, :HEAD_DIM], sb_prev, over) + dot(own[:, :HEAD_DIM], sb_own, over)) * SCALE
    ).astype(BF)
    grads[64:128, :] = (
        (dot(q, sb_own, across) + live * dot(q_next, sb_next, across)) * SCALE
    ).astype(BF)
    grads[128:192, :] = (dot(out, p_own, across) + live * dot(out_next, p_next, across)).astype(BF)
    line = rows_of((16, TOK))
    tail = jnp.zeros((16, TOK), F32)
    for k in range(TOPK):
        high = aligned[k : k + 1, :].astype(BF).astype(F32)
        tail = jnp.where(line == k, high, tail)
        tail = jnp.where(line == TOPK + k, aligned[k : k + 1, :] - high, tail)
    grads[192:208, :] = tail.astype(BF)


def expert_kernel(rows, down, gate, up, own_g, own_u, from_prev, from_next, sent, total):
    features = rows[:, :, 0:D].reshape(MINE, D)
    across = ((1,), (1,))

    def act(hidden, g, u):
        g, u = g.astype(F32), u.astype(F32)
        sigma = jax.nn.sigmoid(g)
        return (
            (hidden * u * (sigma * (1.0 + g * (1.0 - sigma)))).astype(BF),
            (hidden * (g * sigma)).astype(BF),
        )

    def stored(ref, n):
        return jnp.concatenate(
            [ref[3 * HALF :, (3 * n + m) * MINE : (3 * n + m + 1) * MINE] for m in range(3)], axis=0
        )

    backs = list(act(dot(down[...], features, across), own_g[...], own_u[...]))
    for ref in (from_prev, from_next):
        backs += list(act(dot(ref[0:HALF, :], features, across), stored(ref, 0), stored(ref, 1)))
    weights = [gate[...], up[...]]
    for ref in (from_prev, from_next):
        weights += [ref[HALF : 2 * HALF, :], ref[2 * HALF : 3 * HALF, :]]
    total[0:D, :] = dot(
        jnp.concatenate(weights, axis=0), jnp.concatenate(backs, axis=0), ((0,), (0,))
    )
    total[D:, :] = jnp.zeros((8, MINE), F32)
    for c in range(32):
        sent[c, :, :] = total[c * COLS : c * COLS + PART, :].astype(BF)


def combine_kernel(returned, places, sent):
    slot = rows_of((CAP, TOK)).astype(F32)
    empty = jnp.zeros((CAP, TOK), BF)
    for h in range(2):
        total = jnp.zeros((PART, 4 * TOK), F32)
        for pair in range(0, EXPERTS, 2):
            picks = []
            for e in (pair, pair + 1):
                for b in range(4):
                    lanes = slice((4 * h + b) * TOK, (4 * h + b + 1) * TOK)
                    pick = (slot == places[e : e + 1, lanes]).astype(BF)
                    picks.append(jnp.concatenate([empty] * b + [pick] + [empty] * (3 - b), axis=1))
            terms = [returned[e, :, h * TOK : (h + 1) * TOK] for e in (pair, pair + 1)]
            total = total + dot(jnp.concatenate(terms, axis=1), jnp.concatenate(picks, axis=0))
        for b in range(4):
            sent[4 * h + b, :, :] = total[:, b * TOK : (b + 1) * TOK].astype(BF)


def project_kernel(grads, rows, key_w, value_w, router, shares, routes, attended):
    total = jnp.zeros((PART, TOK), F32)
    for h in range(QH):
        for n in range(2):
            weight = rows[h, :, n * 128 : n * 128 + PART]
            total = total + dot(weight, grads[h, 32 * n : 32 * n + 32, :], ((0,), (0,)))
    group = QH // KVH
    for first, weight in ((64, key_w), (128, value_w)):
        sums = []
        for g in range(KVH):
            some = grads[g * group, first : first + 64, :].astype(F32)
            for h in range(g * group + 1, (g + 1) * group):
                some = some + grads[h, first : first + 64, :].astype(F32)
            sums.append(some)
        high, low = split(jnp.concatenate(sums, axis=0))
        total = total + dot(weight[...], high) + dot(weight[...], low)
    tail = grads[0, 192:208, :].astype(F32)
    for h in range(1, QH):
        tail = tail + grads[h, 192:208, :].astype(F32)
    aligned = [tail[k : k + 1, :] + tail[TOPK + k : TOPK + k + 1, :] for k in range(TOPK)]
    mean = sum(shares[k : k + 1, :] * aligned[k] for k in range(TOPK))
    names = rows_of((EXPERTS, TOK))
    coef = jnp.zeros((EXPERTS, TOK), F32)
    for k in range(TOPK):
        back = shares[k : k + 1, :] * (aligned[k] - mean)
        coef = jnp.where(names == routes[k : k + 1, :], back, coef)
    high, low = split(coef)
    attended[...] = total + dot(router[...], high) + dot(router[...], low)


def lift_kernel(bands, attended, gain, values, lifted, stat):
    total = attended[...]
    for b in range(BLOCKS):
        total = total + bands[b, :, :].astype(F32)
    total = jnp.where(rows_of((PART, TOK)) < COLS, total, 0.0) * gain[...]
    lifted[...] = total
    stat[...] = jnp.broadcast_to(
        jnp.sum(values[...] * total, axis=0, keepdims=True), (32, TOK)
    )


def finish_kernel(stats, lifted, values, inverse, base, result):
    mean = jnp.sum(stats[...], axis=0, keepdims=True) / D
    inv = inverse[...]
    result[...] = base[...] + (
        inv * lifted[0:COLS, :] - values[0:COLS, :] * (inv * inv * inv * mean)
    )


def on_device(
    adjoint,
    seed_grad,
    layer_input,
    norm_gain,
    router_weight,
    routes,
    expert_out,
    stored_query,
    stored_key,
    stored_value,
    query_weight,
    key_weight,
    value_weight,
    output_weight,
    gate_weight,
    up_weight,
    down_weight,
    stored_gate,
    stored_up,
):
    col = lax.axis_index("exp")
    block = lax.axis_index(SEQ)
    parity = lax.axis_index("zl")
    where = jnp.stack([col, parity, block]).astype(jnp.int32)
    first = col * COLS
    adjoint_t, layer_t, routes_t, router_t = adjoint.T, layer_input.T, routes.T, router_weight.T
    to_next = [(i, (i + 1) % 16) for i in range(16)]
    to_prev = [(j, i) for i, j in to_next]

    pay, inverse, shares, out_back = run(
        route_kernel,
        "route",
        (where, layer_t, norm_gain, router_t, routes_t, adjoint_t, output_weight),
        [((CAP, WIDE), BF), ((1, TOK), F32), ((TOPK, TOK), F32), ((HEAD_DIM, TOK), BF)],
        room=60,
    )
    gathered = lax.all_gather(pay, "zh", axis=0)

    down, gate, up = down_weight[0], gate_weight[0].T, up_weight[0].T
    wide, narrow = ((3 * HALF + 16, D), BF), ((BAND, MINE), BF)
    w_next, w_prev, own_g, own_u = run(
        pack_kernel,
        "pack",
        (where, down, gate, up, stored_gate[0].T, stored_up[0].T),
        [wide, wide, narrow, narrow],
    )

    w_next, w_prev, query_weight = lax.optimization_barrier((w_next, w_prev, query_weight))
    w_from_prev = lax.ppermute(w_next, SEQ, to_next)
    w_from_next = lax.ppermute(w_prev, SEQ, to_prev)

    (query_parts,) = run(share_kernel, "share", (query_weight.T,), [((32, 32, 256), BF)])
    query_cols = lax.all_to_all(query_parts, "exp", 0, 0, tiled=True)
    kv_start = col // (QH // KVH) * HEAD_DIM
    kv = jnp.concatenate(
        [lax.dynamic_slice_in_dim(a, kv_start, HEAD_DIM, 1) for a in (stored_key, stored_value)], axis=1
    )
    query_t = stored_query.T
    kv_prev = lax.ppermute(kv, SEQ, to_next)
    from_next_q = lax.ppermute(jnp.concatenate([query_t, out_back, kv], axis=0), SEQ, to_prev)
    kv_prev, from_next_q, w_from_prev, w_from_next = lax.optimization_barrier(
        (kv_prev, from_next_q, w_from_prev, w_from_next)
    )
    adjoint_cols = lax.dynamic_slice_in_dim(adjoint_t, first, COLS, 0).astype(F32)
    values = lax.dynamic_slice_in_dim(layer_t, first, COLS, 0).astype(F32)
    aligned = jnp.sum(adjoint_cols[:, None, :] * expert_out.transpose(2, 1, 0).astype(F32), axis=0)
    (grads,) = run(
        attend_kernel,
        "attend",
        (where, query_t, out_back, kv, kv_prev, from_next_q, aligned),
        [((208, TOK), BF)],
    )
    gathered, grads, query_cols = lax.optimization_barrier((gathered, grads, query_cols))
    all_grads = lax.all_gather(grads, "exp", axis=0)
    (terms,) = run(
        expert_kernel,
        "expert",
        (gathered, down, gate, up, own_g, own_u, w_from_prev, w_from_next),
        [((32, PART, MINE), BF)],
        [pltpu.VMEM((D + 8, MINE), F32)],
        room=32,
    )
    returned = lax.all_to_all(terms, "exp", 0, 0, tiled=True)
    (places,) = run(
        slots_kernel, "slots", (gathered[:, 0:16, D:],), [((EXPERTS, BLOCKS * TOK), F32)]
    )
    (sums,) = run(combine_kernel, "combine", (returned, places), [((BLOCKS, PART, TOK), BF)])
    bands = lax.all_to_all(sums, "zh", 0, 0, tiled=True)

    pad = ((0, PART - COLS), (0, 0))
    router_cols = jnp.pad(lax.dynamic_slice_in_dim(router_weight, first, COLS, 0), pad)
    (attended,) = run(
        project_kernel,
        "project",
        (all_grads, query_cols, jnp.pad(key_weight, pad), jnp.pad(value_weight, pad), router_cols, shares, routes_t),
        [((PART, TOK), F32)],
    )
    gain = jnp.pad(lax.dynamic_slice_in_dim(norm_gain, first, COLS, 0)[:, None], pad)
    values = jnp.pad(values, pad)
    lifted, stat = run(
        lift_kernel, "lift", (bands, attended, gain, values), [((PART, TOK), F32), ((32, TOK), F32)]
    )
    stats = lax.all_to_all(stat, "exp", 0, 0, tiled=True)
    (result,) = run(
        finish_kernel,
        "finish",
        (stats, lifted, values, inverse, seed_grad.T + adjoint_cols),
        [((COLS, TOK), F32)],
    )
    return result.T


def solution(mesh):
    finer = Mesh(mesh.devices.reshape(8, 2, 32), ("zh", "zl", "exp"))
    placed = (
        P(SEQ, None),
        P(SEQ, "exp"),
        P(SEQ, None),
        P(),
        P(),
        P(SEQ, None),
        P(SEQ, None, "exp"),
        P(SEQ, "exp"),
        P(SEQ, None),
        P(SEQ, None),
        P(None, "exp"),
        P("exp", None),
        P("exp", None),
        P("exp", None),
        P("exp", None, SEQ),
        P("exp", None, SEQ),
        P("exp", SEQ, None),
        P("exp", None, SEQ),
        P("exp", None, SEQ),
    )
    return jax.shard_map(
        on_device, mesh=finer, in_specs=placed, out_specs=P(SEQ, "exp"), check_vma=False
    )
```
